32 devices in a mesh: parts: 2 (over x), dp: 4 (over z), tensor: 4 (over y, core).
Axes of the slice: x: 2, y: 2, z: 4, core: 2. Of those that a mesh axis runs over, the one named last changes fastest.
Arguments:
- activations: bfloat16 [8, 128, 4096], P(('parts', 'dp'), None, 'tensor'), parts along dimension 0, may hold values from -6 to 6
- out_grad: bfloat16 [8, 128, 4096], P(('parts', 'dp'), None, 'tensor'), parts along dimension 0, may hold values from -2.5 to 2.5
- w_gate: bfloat16 [28672, 4096], P(('parts', 'dp', 'tensor')), parts along dimension 0, may hold values from -0.09375 to 0.09375
- w_up: bfloat16 [28672, 4096], P(('parts', 'dp', 'tensor')), parts along dimension 0, may hold values from -0.09375 to 0.09375
- w_down: bfloat16 [28672, 4096], P(('parts', 'dp', 'tensor')), parts along dimension 0, may hold values from -0.09375 to 0.09375
Outputs:
- fisher_gate: float32 [28672, 4096], P(('parts', 'dp', 'tensor')), parts along dimension 0
- fisher_up: float32 [28672, 4096], P(('parts', 'dp', 'tensor')), parts along dimension 0
- fisher_down: float32 [28672, 4096], P(('parts', 'dp', 'tensor')), parts along dimension 0
The draws below stay inside these ranges and needn't reach their ends.
There are 2 independent parts, one for each index of `parts`. The reference program is written for one: setup_inputs(seed, part) draws one part's arguments, and reference() takes and returns one part's arrays. A program takes and returns all parts, laid end to end along the dimension named above; each array names one. Nothing has to cross between parts.
All inputs are finite; a program needn't handle non-finite values.
Results may differ from the reference program's by a relative error of at most 0.0037.
Values may be sent and summed in bfloat16 or wider, within the bound.
A program may use at most 192 MiB of HBM per device.

```python
import jax
import jax.numpy as jnp
from jax import lax

D = 4096
FF = 14336
SEQ = 128
EXAMPLES = 4


def level_of(key, shape, split, smallest, high):
    level, own = 1.0, jax.random.fold_in(key, 6)
    for dim, parts in split:
        heights = jnp.exp(jax.random.uniform(jax.random.fold_in(own, dim), (parts,), jnp.float32, smallest / len(split), high / len(split)))
        level = level * jnp.repeat(heights, shape[dim] // parts).reshape([-1 if axis == dim else 1 for axis in range(len(shape))])
    return level


def scatter_about(own_key, extent, scale, bound, split=(), kind=jnp.bfloat16):
    entries = scale * jax.random.normal(own_key, extent, jnp.float32)
    if split:
        entries = entries * level_of(own_key, extent, split, -0.22, 0.18)
    return jnp.clip(entries, -bound, bound).astype(kind)


def setup_inputs(seed: int = 0, part: int = 0) -> dict:
    streams_of = jax.random.split(jax.random.key(seed), 6)
    part_splits = jax.random.split(jax.random.fold_in(streams_of[5], part), 6)
    return {
        "activations": scatter_about(part_splits[0], (EXAMPLES, SEQ, D), 1.0, 6.0, ((0, 4), (2, 4))),
        "out_grad": scatter_about(part_splits[1], (EXAMPLES, SEQ, D), 0.18, 2.5, ((0, 4), (2, 4))),
        "w_gate": scatter_about(part_splits[2], (FF, D), D ** -0.5, 0.09375, ((0, 16),)),
        "w_up": scatter_about(part_splits[3], (FF, D), D ** -0.5, 0.09375, ((0, 16),)),
        "w_down": scatter_about(part_splits[4], (FF, D), D ** -0.5, 0.09375, ((0, 16),)),
    }


def example_terms(totals, x_ex, y_ex, w_gate, w_up, w_down):
    dims = (((1,), (1,)), ((), ()))
    gate_pre = lax.dot_general(w_gate, x_ex, dims, preferred_element_type=jnp.float32)
    up_pre = lax.dot_general(w_up, x_ex, dims, preferred_element_type=jnp.float32)
    sig_gate = jax.nn.sigmoid(gate_pre)
    silu_gate = gate_pre * sig_gate
    hidden = (silu_gate * up_pre).astype(jnp.bfloat16)
    grad_hidden = lax.dot_general(w_down, y_ex, dims, preferred_element_type=jnp.float32)
    grad_gate = (grad_hidden * up_pre * sig_gate * (1.0 + gate_pre * (1.0 - sig_gate))).astype(jnp.bfloat16)
    grad_up = (grad_hidden * silu_gate).astype(jnp.bfloat16)
    g_gate = jnp.dot(grad_gate, x_ex, preferred_element_type=jnp.float32)
    g_up = jnp.dot(grad_up, x_ex, preferred_element_type=jnp.float32)
    g_down = jnp.dot(hidden, y_ex, preferred_element_type=jnp.float32)
    return (totals[0] + g_gate * g_gate, totals[1] + g_up * g_up, totals[2] + g_down * g_down)


def reference(activations, out_grad, w_gate, w_up, w_down):
    count = activations.shape[0]
    empty = jnp.zeros(w_gate.shape, jnp.float32)

    def step_fn(step_index, totals):
        x_ex = lax.dynamic_index_in_dim(activations, step_index, 0, keepdims=False)
        y_ex = lax.dynamic_index_in_dim(out_grad, step_index, 0, keepdims=False)
        return example_terms(totals, x_ex, y_ex, w_gate, w_up, w_down)

    totals = lax.fori_loop(0, count, step_fn, (empty, empty, empty))
    return (totals[0] / count, totals[1] / count, totals[2] / count)
```

```python
import functools

import jax
import jax.numpy as jnp
from jax import lax
from jax.experimental import pallas as pl
from jax.experimental.pallas import tpu as pltpu
from jax.sharding import PartitionSpec as P

MESH = pl.DeviceIdType.MESH
NT = (((1,), (1,)), ((), ()))


def row_chunk(rows, most):
    return max(r for r in range(16, most + 1, 16) if rows % r == 0)


def gather_forward(
    n_dp, n_tensor,
    x_ref, y_ref, wg_ref, wu_ref, wd_ref,
    xo_ref, yo_ref, gg_ref, gu_ref, hid_ref,
    xb, yb, wg, wu, wd, gate, up,
    own_sem, w_sem, recv_sem, line_sem, sib_sem, out_sem,
):
    z, t = lax.axis_index("dp"), lax.axis_index("tensor")
    core = lax.rem(t, 2)
    line = t // 2
    n_lines = n_tensor // 2
    unit = x_ref.shape[0]
    depth = x_ref.shape[1]
    rows = wg.shape[0]
    bufs = (xb, yb)

    weights = [
        pltpu.make_async_copy(src, dst, w_sem.at[i])
        for i, (src, dst) in enumerate(((wg_ref, wg), (wu_ref, wu), (wd_ref, wd)))
    ]
    own = [
        pltpu.make_async_copy(
            src, bufs[a].at[t, pl.ds(z * unit, unit), :], own_sem.at[a]
        )
        for a, src in enumerate((x_ref, y_ref))
    ]
    for copy in own:
        copy.start()

    barrier = pltpu.get_barrier_semaphore()
    has_up, has_down = z < n_dp - 1, z > 0

    @pl.when(has_up)
    def _():
        pl.semaphore_signal(barrier, 1, device_id={"dp": z + 1}, device_id_type=MESH)

    @pl.when(has_down)
    def _():
        pl.semaphore_signal(barrier, 1, device_id={"dp": z - 1}, device_id_type=MESH)

    def peer(j):
        return lax.rem(line + j, n_lines) * 2 + core

    for j in range(1, n_lines):
        pl.semaphore_signal(barrier, 1, device_id={"tensor": peer(j)}, device_id_type=MESH)
    sibling = line * 2 + 1 - core
    pl.semaphore_signal(barrier, 1, device_id={"tensor": sibling}, device_id_type=MESH)
    pl.semaphore_wait(
        barrier, n_lines + has_up.astype(jnp.int32) + has_down.astype(jnp.int32)
    )
    for copy in own:
        copy.wait()

    sent = []

    def slot(a, zz, tt):
        return bufs[a].at[tt, pl.ds(zz * unit, unit), :]

    def push(a, zz, tt, sem, target, cond):
        copy = pltpu.make_async_remote_copy(
            src_ref=slot(a, zz, tt),
            dst_ref=slot(a, zz, tt),
            send_sem=sem,
            recv_sem=recv_sem.at[a, zz, tt],
            device_id=target,
            device_id_type=MESH,
        )
        if cond is None:
            copy.start()
            sent.append(copy.wait_send)
        else:
            pl.when(cond)(copy.start)
            sent.append(lambda: pl.when(cond)(copy.wait_send))

    def arrived(a, zz, tt):
        pltpu.make_async_copy(slot(a, zz, tt), slot(a, zz, tt), recv_sem.at[a, zz, tt]).wait()

    def guarded(cond, do):
        if cond is None:
            do()
        else:
            pl.when(cond)(do)

    def both(*conds):
        conds = [c for c in conds if c is not None]
        return functools.reduce(jnp.logical_and, conds) if conds else None

    def on_line(a, k):
        for sign in (1, -1) if k else (0,):
            zz = z - sign * k
            cond = None if k == 0 else (zz >= 0 if sign > 0 else zz < n_dp)
            safe = jnp.clip(zz, 0, n_dp - 1)
            if k:
                guarded(cond, lambda: arrived(a, safe, t))
            if sign >= 0:
                push(a, safe, t, line_sem.at[a, safe, 0], {"dp": z + 1}, both(cond, has_up))
            if sign <= 0:
                push(a, safe, t, line_sem.at[a, safe, 1], {"dp": z - 1}, both(cond, has_down))
            for j in range(1, n_lines):
                push(a, safe, t, line_sem.at[a, safe, 1 + j], {"tensor": peer(j)}, cond)
            push(a, safe, t, sib_sem.at[a, safe, line], {"tensor": sibling}, cond)

    def from_peers(a, k):
        for sign in (1, -1) if k else (0,):
            zz = z - sign * k
            cond = None if k == 0 else (zz >= 0 if sign > 0 else zz < n_dp)
            safe = jnp.clip(zz, 0, n_dp - 1)
            for j in range(1, n_lines):
                tt = peer(j)
                guarded(cond, lambda: arrived(a, safe, tt))
                push(a, safe, tt, sib_sem.at[a, safe, tt // 2], {"tensor": sibling}, cond)

    def from_sibling(a):
        for zz in range(n_dp):
            for l in range(n_lines):
                arrived(a, zz, 2 * l + 1 - core)

    chunk = row_chunk(rows, 448)

    def project(w, act, acc, k):
        @pl.loop(0, rows // chunk)
        def _(i):
            r = pl.ds(pl.multiple_of(i * chunk, chunk), chunk)
            part = lax.dot_general(
                w[r, k * depth:(k + 1) * depth], act[k], NT,
                preferred_element_type=jnp.float32,
            )
            if k == 0:
                acc[r, :] = part
            else:
                acc[r, :] += part

    on_line(0, 0)
    for copy in weights:
        copy.start()
    half = max(1, n_dp // 2)
    for k in range(1, n_dp):
        if k == half:
            on_line(1, 0)
        on_line(0, k)
        from_peers(0, k - 1)
    if n_dp == 1:
        on_line(1, 0)
    from_peers(0, n_dp - 1)
    on_line(1, 1)
    from_sibling(0)
    x_out = pltpu.make_async_copy(xb, xo_ref, out_sem.at[0])
    x_out.start()
    weights[0].wait()
    weights[1].wait()
    steps = [(w, acc, k) for k in range(n_tensor) for w, acc in ((wg, gate), (wu, up))]
    done = 0
    for k in range(2, n_dp):
        upto = len(steps) * (k - 1) // (n_dp - 2)
        for w, acc, kk in steps[done:upto]:
            project(w, xb, acc, kk)
        done = upto
        on_line(1, k)
        from_peers(1, k - 2)
    for w, acc, kk in steps[done:]:
        project(w, xb, acc, kk)

    small = row_chunk(rows, 64)

    @pl.loop(0, rows // small)
    def _(i):
        r = pl.ds(pl.multiple_of(i * small, small), small)
        g, u = gate[r, :], up[r, :]
        sig = jax.nn.sigmoid(g)
        silu = g * sig
        hid_ref[r, :] = (silu * u).astype(jnp.bfloat16)
        gate[r, :] = u * sig * (1.0 + g * (1.0 - sig))
        up[r, :] = silu

    from_peers(1, n_dp - 2)
    from_peers(1, n_dp - 1)
    from_sibling(1)
    y_out = pltpu.make_async_copy(yb, yo_ref, out_sem.at[1])
    y_out.start()
    weights[2].wait()

    width = n_tensor

    @pl.loop(0, rows // chunk)
    def _(i):
        r = pl.ds(pl.multiple_of(i * chunk, chunk), chunk)
        grad = lax.dot_general(wd[r, :depth], yb[0], NT, preferred_element_type=jnp.float32)
        for k in range(1, width):
            grad += lax.dot_general(
                wd[r, k * depth:(k + 1) * depth], yb[k], NT,
                preferred_element_type=jnp.float32,
            )
        gg_ref[r, :] = (grad * gate[r, :]).astype(jnp.bfloat16)
        gu_ref[r, :] = (grad * up[r, :]).astype(jnp.bfloat16)

    for wait in sent:
        wait()
    x_out.wait()
    y_out.wait()


def squares(count, seq, gg_ref, gu_ref, hid_ref, x_ref, y_ref, fg_ref, fu_ref, fd_ref):
    rows, columns = fg_ref.shape
    chunk = row_chunk(rows, 448)
    wide = 256 if columns % 256 == 0 else columns
    for act, grads, out in ((x_ref, gg_ref, fg_ref), (x_ref, gu_ref, fu_ref), (y_ref, hid_ref, fd_ref)):
        for q in range(columns // wide):
            @pl.loop(0, rows // chunk)
            def _(i):
                r = pl.ds(pl.multiple_of(i * chunk, chunk), chunk)
                total = None
                for e in range(count):
                    span = slice(e * seq, (e + 1) * seq)
                    g = jnp.dot(
                        grads[r, span], act[span, q * wide:(q + 1) * wide],
                        preferred_element_type=jnp.float32,
                    )
                    total = g * g if total is None else total + g * g
                out[r, q * wide:(q + 1) * wide] = total * (1.0 / count)


def local(n_dp, n_tensor, activations, out_grad, w_gate, w_up, w_down):
    per, seq, depth = activations.shape
    count = per * n_dp
    rows, features = w_gate.shape
    tokens = count * seq
    x = activations.reshape(per * seq, depth)
    y = out_grad.reshape(per * seq, depth)
    n_lines = n_tensor // 2
    blocks = jax.ShapeDtypeStruct((n_tensor, tokens, depth), jnp.bfloat16)
    grads = jax.ShapeDtypeStruct((rows, tokens), jnp.bfloat16)
    anywhere = pl.BlockSpec(memory_space=pl.ANY)
    in_vmem = pl.BlockSpec(memory_space=pltpu.VMEM)
    xb, yb, gg, gu, hid = pl.pallas_call(
        functools.partial(gather_forward, n_dp, n_tensor),
        out_shape=(blocks, blocks, grads, grads, grads),
        in_specs=[anywhere] * 5,
        out_specs=(anywhere, anywhere, in_vmem, in_vmem, in_vmem),
        scratch_shapes=[
            pltpu.VMEM(blocks.shape, jnp.bfloat16),
            pltpu.VMEM(blocks.shape, jnp.bfloat16),
            pltpu.VMEM((rows, features), jnp.bfloat16),
            pltpu.VMEM((rows, features), jnp.bfloat16),
            pltpu.VMEM((rows, features), jnp.bfloat16),
            pltpu.VMEM((rows, tokens), jnp.float32),
            pltpu.VMEM((rows, tokens), jnp.float32),
            pltpu.SemaphoreType.DMA((2,)),
            pltpu.SemaphoreType.DMA((3,)),
            pltpu.SemaphoreType.DMA((2, n_dp, n_tensor)),
            pltpu.SemaphoreType.DMA((2, n_dp, 1 + n_lines)),
            pltpu.SemaphoreType.DMA((2, n_dp, n_lines)),
            pltpu.SemaphoreType.DMA((2,)),
        ],
        compiler_params=pltpu.CompilerParams(
            collective_id=0, has_side_effects=True, vmem_limit_bytes=56 * 2**20
        ),
        name="gather_forward",
    )(x, y, w_gate, w_up, w_down)

    wide = min(depth, 512)
    per_block = depth // wide
    whole = pl.BlockSpec((rows, tokens), lambda i: (0, 0))
    act_spec = pl.BlockSpec((None, tokens, wide), lambda i: (i // per_block, 0, i % per_block))
    out_spec = pl.BlockSpec((rows, wide), lambda i: (0, i))
    fisher = jax.ShapeDtypeStruct((rows, features), jnp.float32)
    return pl.pallas_call(
        functools.partial(squares, count, seq),
        grid=(features // wide,),
        out_shape=(fisher, fisher, fisher),
        in_specs=[whole, whole, whole, act_spec, act_spec],
        out_specs=(out_spec, out_spec, out_spec),
        compiler_params=pltpu.CompilerParams(vmem_limit_bytes=56 * 2**20),
        name="squares",
    )(gg, gu, hid, xb, yb)


def solution(mesh):
    n_dp, n_tensor = mesh.shape["dp"], mesh.shape["tensor"]
    return jax.shard_map(
        functools.partial(local, n_dp, n_tensor),
        mesh=mesh,
        in_specs=(
            P(("parts", "dp"), None, "tensor"),
            P(("parts", "dp"), None, "tensor"),
            P(("parts", "dp", "tensor"), None),
            P(("parts", "dp", "tensor"), None),
            P(("parts", "dp", "tensor"), None),
        ),
        out_specs=(
            P(("parts", "dp", "tensor"), None),
            P(("parts", "dp", "tensor"), None),
            P(("parts", "dp", "tensor"), None),
        ),
        check_vma=False,
    )
```

```python
import functools

import jax
import jax.numpy as jnp
from jax import lax
from jax.experimental import pallas as pl
from jax.experimental.pallas import tpu as pltpu
from jax.sharding import PartitionSpec as P

MESH = pl.DeviceIdType.MESH
NT = (((1,), (1,)), ((), ()))


def row_chunk(rows, most):
    return max(r for r in range(16, most + 1, 16) if rows % r == 0)


def gather_forward(
    n_dp, n_tensor,
    x_ref, y_ref, wg_ref, wu_ref, wd_ref,
    xo_ref, yo_ref, gg_ref, gu_ref, hid_ref,
    xb, yb, wg, wu, wd, gate, up,
    own_sem, w_sem, recv_sem, line_sem, sib_sem, out_sem,
):
    z, t = lax.axis_index("dp"), lax.axis_index("tensor")
    core = lax.rem(t, 2)
    line = t // 2
    n_lines = n_tensor // 2
    unit = x_ref.shape[0]
    depth = x_ref.shape[1]
    rows = wg.shape[0]
    bufs = (xb, yb)

    weights = [
        pltpu.make_async_copy(src, dst, w_sem.at[i])
        for i, (src, dst) in enumerate(((wg_ref, wg), (wu_ref, wu), (wd_ref, wd)))
    ]
    own = [
        pltpu.make_async_copy(
            src, bufs[a].at[t, pl.ds(z * unit, unit), :], own_sem.at[a]
        )
        for a, src in enumerate((x_ref, y_ref))
    ]
    for copy in own:
        copy.start()

    barrier = pltpu.get_barrier_semaphore()
    has_up, has_down = z < n_dp - 1, z > 0

    @pl.when(has_up)
    def _():
        pl.semaphore_signal(barrier, 1, device_id={"dp": z + 1}, device_id_type=MESH)

    @pl.when(has_down)
    def _():
        pl.semaphore_signal(barrier, 1, device_id={"dp": z - 1}, device_id_type=MESH)

    def peer(j):
        return lax.rem(line + j, n_lines) * 2 + core

    for j in range(1, n_lines):
        pl.semaphore_signal(barrier, 1, device_id={"tensor": peer(j)}, device_id_type=MESH)
    sibling = line * 2 + 1 - core
    pl.semaphore_signal(barrier, 1, device_id={"tensor": sibling}, device_id_type=MESH)
    pl.semaphore_wait(
        barrier, n_lines + has_up.astype(jnp.int32) + has_down.astype(jnp.int32)
    )
    for copy in own:
        copy.wait()

    sent = []

    def slot(a, zz, tt):
        return bufs[a].at[tt, pl.ds(zz * unit, unit), :]

    def push(a, zz, tt, sem, target, cond):
        copy = pltpu.make_async_remote_copy(
            src_ref=slot(a, zz, tt),
            dst_ref=slot(a, zz, tt),
            send_sem=sem,
            recv_sem=recv_sem.at[a, zz, tt],
            device_id=target,
            device_id_type=MESH,
        )
        if cond is None:
            copy.start()
            sent.append(copy.wait_send)
        else:
            pl.when(cond)(copy.start)
            sent.append(lambda: pl.when(cond)(copy.wait_send))

    def arrived(a, zz, tt):
        pltpu.make_async_copy(slot(a, zz, tt), slot(a, zz, tt), recv_sem.at[a, zz, tt]).wait()

    def guarded(cond, do):
        if cond is None:
            do()
        else:
            pl.when(cond)(do)

    def both(*conds):
        conds = [c for c in conds if c is not None]
        return functools.reduce(jnp.logical_and, conds) if conds else None

    def on_line(a, k):
        for sign in (1, -1) if k else (0,):
            zz = z - sign * k
            cond = None if k == 0 else (zz >= 0 if sign > 0 else zz < n_dp)
            safe = jnp.clip(zz, 0, n_dp - 1)
            if k:
                guarded(cond, lambda: arrived(a, safe, t))
            if sign >= 0:
                push(a, safe, t, line_sem.at[a, safe, 0], {"dp": z + 1}, both(cond, has_up))
            if sign <= 0:
                push(a, safe, t, line_sem.at[a, safe, 1], {"dp": z - 1}, both(cond, has_down))
            for j in range(1, n_lines):
                push(a, safe, t, line_sem.at[a, safe, 1 + j], {"tensor": peer(j)}, cond)
            push(a, safe, t, sib_sem.at[a, safe, line], {"tensor": sibling}, cond)

    def from_peers(a, k):
        for sign in (1, -1) if k else (0,):
            zz = z - sign * k
            cond = None if k == 0 else (zz >= 0 if sign > 0 else zz < n_dp)
            safe = jnp.clip(zz, 0, n_dp - 1)
            for j in range(1, n_lines):
                tt = peer(j)
                guarded(cond, lambda: arrived(a, safe, tt))
                push(a, safe, tt, sib_sem.at[a, safe, tt // 2], {"tensor": sibling}, cond)

    def from_sibling(a, first, number):
        for i in range(number):
            for l in range(n_lines):
                arrived(a, first + i, 2 * l + 1 - core)

    chunk = row_chunk(rows, 448)

    def project(w, act, acc, k):
        for i in range(rows // chunk):
            r = slice(i * chunk, (i + 1) * chunk)
            part = lax.dot_general(
                w[r, k * depth:(k + 1) * depth], act[k], NT,
                preferred_element_type=jnp.float32,
            )
            if k == 0:
                acc[r, :] = part
            else:
                acc[r, :] += part

    on_line(0, 0)
    for copy in weights:
        copy.start()
    half = max(1, n_dp // 2)
    for k in range(1, n_dp):
        if k == half:
            on_line(1, 0)
        on_line(0, k)
        from_peers(0, k - 1)
    if n_dp == 1:
        on_line(1, 0)
    from_peers(0, n_dp - 1)
    on_line(1, 1)
    from_sibling(0, 0, n_dp)
    x_out = pltpu.make_async_copy(xb, xo_ref, out_sem.at[0])
    x_out.start()
    weights[0].wait()
    weights[1].wait()
    steps = [(w, acc, k) for k in range(n_tensor) for w, acc in ((wg, gate), (wu, up))]
    done = 0
    for k in range(2, n_dp):
        upto = len(steps) * (k - 1) // (n_dp - 2)
        for w, acc, kk in steps[done:upto]:
            project(w, xb, acc, kk)
        done = upto
        on_line(1, k)
        from_peers(1, k - 2)
    for w, acc, kk in steps[done:]:
        project(w, xb, acc, kk)

    small = row_chunk(rows, 64)

    @pl.loop(0, rows // small)
    def _(i):
        r = pl.ds(pl.multiple_of(i * small, small), small)
        g, u = gate[r, :], up[r, :]
        sig = jax.nn.sigmoid(g)
        silu = g * sig
        hid_ref[r, :] = (silu * u).astype(jnp.bfloat16)
        gate[r, :] = u * sig * (1.0 + g * (1.0 - sig))
        up[r, :] = silu

    weights[2].wait()
    parts = 2 if n_dp % 2 == 0 and n_dp > 2 else 1
    size = n_dp // parts

    def backward(first):
        span = pl.ds(pl.multiple_of(first * unit, unit), size * unit)
        for i in range(rows // chunk):
            r = slice(i * chunk, (i + 1) * chunk)
            grad = lax.dot_general(
                wd[r, :depth], yb[0, span, :], NT, preferred_element_type=jnp.float32
            )
            for k in range(1, n_tensor):
                grad += lax.dot_general(
                    wd[r, k * depth:(k + 1) * depth], yb[k, span, :], NT,
                    preferred_element_type=jnp.float32,
                )
            gg_ref[r, span] = (grad * gate[r, span]).astype(jnp.bfloat16)
            gu_ref[r, span] = (grad * up[r, span]).astype(jnp.bfloat16)

    near = (z // size) * size
    if parts == 2:
        from_sibling(1, near, size)
        backward(near)
    from_peers(1, n_dp - 2)
    from_peers(1, n_dp - 1)
    far = size - near if parts == 2 else near
    from_sibling(1, far, size)
    y_out = pltpu.make_async_copy(yb, yo_ref, out_sem.at[1])
    y_out.start()
    backward(far)

    for wait in sent:
        wait()
    x_out.wait()
    y_out.wait()


def squares(count, seq, gg_ref, gu_ref, hid_ref, x_ref, y_ref, fg_ref, fu_ref, fd_ref):
    rows, columns = fg_ref.shape
    chunk = row_chunk(rows, 448)
    wide = 256 if columns % 256 == 0 else columns
    for act, grads, out in ((x_ref, gg_ref, fg_ref), (x_ref, gu_ref, fu_ref), (y_ref, hid_ref, fd_ref)):
        for q in range(columns // wide):
            for i in range(rows // chunk):
                r = slice(i * chunk, (i + 1) * chunk)
                total = None
                for e in range(count):
                    span = slice(e * seq, (e + 1) * seq)
                    g = jnp.dot(
                        grads[r, span], act[span, q * wide:(q + 1) * wide],
                        preferred_element_type=jnp.float32,
                    )
                    total = g * g if total is None else total + g * g
                out[r, q * wide:(q + 1) * wide] = total * (1.0 / count)


def local(n_dp, n_tensor, activations, out_grad, w_gate, w_up, w_down):
    per, seq, depth = activations.shape
    count = per * n_dp
    rows, features = w_gate.shape
    tokens = count * seq
    x = activations.reshape(per * seq, depth)
    y = out_grad.reshape(per * seq, depth)
    n_lines = n_tensor // 2
    blocks = jax.ShapeDtypeStruct((n_tensor, tokens, depth), jnp.bfloat16)
    grads = jax.ShapeDtypeStruct((rows, tokens), jnp.bfloat16)
    anywhere = pl.BlockSpec(memory_space=pl.ANY)
    in_vmem = pl.BlockSpec(memory_space=pltpu.VMEM)
    xb, yb, gg, gu, hid = pl.pallas_call(
        functools.partial(gather_forward, n_dp, n_tensor),
        out_shape=(blocks, blocks, grads, grads, grads),
        in_specs=[anywhere] * 5,
        out_specs=(anywhere, anywhere, in_vmem, in_vmem, in_vmem),
        scratch_shapes=[
            pltpu.VMEM(blocks.shape, jnp.bfloat16),
            pltpu.VMEM(blocks.shape, jnp.bfloat16),
            pltpu.VMEM((rows, features), jnp.bfloat16),
            pltpu.VMEM((rows, features), jnp.bfloat16),
            pltpu.VMEM((rows, features), jnp.bfloat16),
            pltpu.VMEM((rows, tokens), jnp.float32),
            pltpu.VMEM((rows, tokens), jnp.float32),
            pltpu.SemaphoreType.DMA((2,)),
            pltpu.SemaphoreType.DMA((3,)),
            pltpu.SemaphoreType.DMA((2, n_dp, n_tensor)),
            pltpu.SemaphoreType.DMA((2, n_dp, 1 + n_lines)),
            pltpu.SemaphoreType.DMA((2, n_dp, n_lines)),
            pltpu.SemaphoreType.DMA((2,)),
        ],
        compiler_params=pltpu.CompilerParams(
            collective_id=0, has_side_effects=True, vmem_limit_bytes=56 * 2**20
        ),
        name="gather_forward",
    )(x, y, w_gate, w_up, w_down)

    wide = min(depth, 512)
    per_block = depth // wide
    whole = pl.BlockSpec((rows, tokens), lambda i: (0, 0))
    act_spec = pl.BlockSpec((None, tokens, wide), lambda i: (i // per_block, 0, i % per_block))
    out_spec = pl.BlockSpec((rows, wide), lambda i: (0, i))
    fisher = jax.ShapeDtypeStruct((rows, features), jnp.float32)
    return pl.pallas_call(
        functools.partial(squares, count, seq),
        grid=(features // wide,),
        out_shape=(fisher, fisher, fisher),
        in_specs=[whole, whole, whole, act_spec, act_spec],
        out_specs=(out_spec, out_spec, out_spec),
        compiler_params=pltpu.CompilerParams(vmem_limit_bytes=56 * 2**20),
        name="squares",
    )(gg, gu, hid, xb, yb)


def solution(mesh):
    n_dp, n_tensor = mesh.shape["dp"], mesh.shape["tensor"]
    return jax.shard_map(
        functools.partial(local, n_dp, n_tensor),
        mesh=mesh,
        in_specs=(
            P(("parts", "dp"), None, "tensor"),
            P(("parts", "dp"), None, "tensor"),
            P(("parts", "dp", "tensor"), None),
            P(("parts", "dp", "tensor"), None),
            P(("parts", "dp", "tensor"), None),
        ),
        out_specs=(
            P(("parts", "dp", "tensor"), None),
            P(("parts", "dp", "tensor"), None),
            P(("parts", "dp", "tensor"), None),
        ),
        check_vma=False,
    )
```

```python
import functools

import jax
import jax.numpy as jnp
from jax import lax
from jax.experimental import pallas as pl
from jax.experimental.pallas import tpu as pltpu
from jax.sharding import PartitionSpec as P

MESH = pl.DeviceIdType.MESH
NT = (((1,), (1,)), ((), ()))


def row_chunk(rows, most):
    return max(r for r in range(16, most + 1, 16) if rows % r == 0)


def gather_forward(
    n_dp, n_tensor,
    x_ref, y_ref, wg_ref, wu_ref, wd_ref,
    xo_ref, yo_ref, gg_ref, gu_ref, hid_ref,
    xb, yb, wg, wu, wd, gate, up,
    own_sem, w_sem, recv_sem, line_sem, sib_sem, pair_sem, out_sem,
):
    z, t = lax.axis_index("dp"), lax.axis_index("tensor")
    core = lax.rem(t, 2)
    line = t // 2
    n_lines = n_tensor // 2
    unit = x_ref.shape[0]
    depth = x_ref.shape[1]
    rows = wg.shape[0]
    bufs = (xb, yb)

    weights = [
        pltpu.make_async_copy(src, dst, w_sem.at[i])
        for i, (src, dst) in enumerate(((wg_ref, wg), (wu_ref, wu), (wd_ref, wd)))
    ]
    own = [
        pltpu.make_async_copy(
            src, bufs[a].at[t, pl.ds(z * unit, unit), :], own_sem.at[a]
        )
        for a, src in enumerate((x_ref, y_ref))
    ]
    for copy in own:
        copy.start()

    barrier = pltpu.get_barrier_semaphore()
    has_up, has_down = z < n_dp - 1, z > 0

    @pl.when(has_up)
    def _():
        pl.semaphore_signal(barrier, 1, device_id={"dp": z + 1}, device_id_type=MESH)

    @pl.when(has_down)
    def _():
        pl.semaphore_signal(barrier, 1, device_id={"dp": z - 1}, device_id_type=MESH)

    def peer(j):
        return lax.rem(line + j, n_lines) * 2 + core

    for j in range(1, n_lines):
        pl.semaphore_signal(barrier, 1, device_id={"tensor": peer(j)}, device_id_type=MESH)
    sibling = line * 2 + 1 - core
    pl.semaphore_signal(barrier, 1, device_id={"tensor": sibling}, device_id_type=MESH)
    pl.semaphore_wait(
        barrier, n_lines + has_up.astype(jnp.int32) + has_down.astype(jnp.int32)
    )
    for copy in own:
        copy.wait()

    sent = []
    paired = n_dp % 2 == 0
    even = lax.rem(z, 2) == 0
    partner = z + 1 - 2 * lax.rem(z, 2)

    def slot(a, zz, tt):
        return bufs[a].at[tt, pl.ds(zz * unit, unit), :]

    def push(a, zz, tt, sem, target, cond):
        copy = pltpu.make_async_remote_copy(
            src_ref=slot(a, zz, tt),
            dst_ref=slot(a, zz, tt),
            send_sem=sem,
            recv_sem=recv_sem.at[a, zz, tt],
            device_id=target,
            device_id_type=MESH,
        )
        if cond is None:
            copy.start()
            sent.append(copy.wait_send)
        else:
            pl.when(cond)(copy.start)
            sent.append(lambda: pl.when(cond)(copy.wait_send))

    def arrived(a, zz, tt):
        pltpu.make_async_copy(slot(a, zz, tt), slot(a, zz, tt), recv_sem.at[a, zz, tt]).wait()

    def guarded(cond, do):
        if cond is None:
            do()
        else:
            pl.when(cond)(do)

    def both(*conds):
        conds = [c for c in conds if c is not None]
        return functools.reduce(jnp.logical_and, conds) if conds else None

    def on_line(a, k):
        for sign in (1, -1) if k else (0,):
            zz = z - sign * k
            cond = None if k == 0 else (zz >= 0 if sign > 0 else zz < n_dp)
            safe = jnp.clip(zz, 0, n_dp - 1)
            if k:
                guarded(cond, lambda: arrived(a, safe, t))
            if sign >= 0:
                push(a, safe, t, line_sem.at[a, safe, 0], {"dp": z + 1}, both(cond, has_up))
            if sign <= 0:
                push(a, safe, t, line_sem.at[a, safe, 1], {"dp": z - 1}, both(cond, has_down))
            for j in range(1, n_lines):
                over = cond
                if a == 1 and k == 1 and paired:
                    over = both(cond, even if sign > 0 else jnp.logical_not(even))
                push(a, safe, t, line_sem.at[a, safe, 1 + j], {"tensor": peer(j)}, over)
            push(a, safe, t, sib_sem.at[a, safe, line], {"tensor": sibling}, cond)

    def from_peers(a, k):
        for sign in (1, -1) if k else (0,):
            zz = z - sign * k
            cond = None if k == 0 else (zz >= 0 if sign > 0 else zz < n_dp)
            safe = jnp.clip(zz, 0, n_dp - 1)
            for j in range(1, n_lines):
                tt = peer(j)
                guarded(cond, lambda: arrived(a, safe, tt))
                if a == 1 and k == 0 and paired:
                    push(a, safe, tt, pair_sem.at[j - 1], {"dp": partner}, None)
                push(a, safe, tt, sib_sem.at[a, safe, tt // 2], {"tensor": sibling}, cond)

    def from_sibling(a, first, number):
        for i in range(number):
            for l in range(n_lines):
                arrived(a, first + i, 2 * l + 1 - core)

    chunk = row_chunk(rows, 448)

    def project(w, act, acc, k):
        for i in range(rows // chunk):
            r = slice(i * chunk, (i + 1) * chunk)
            part = lax.dot_general(
                w[r, k * depth:(k + 1) * depth], act[k], NT,
                preferred_element_type=jnp.float32,
            )
            if k == 0:
                acc[r, :] = part
            else:
                acc[r, :] += part

    on_line(0, 0)
    for copy in weights:
        copy.start()
    half = max(1, n_dp // 2)
    for k in range(1, n_dp):
        if k == half:
            on_line(1, 0)
        on_line(0, k)
        from_peers(0, k - 1)
    if n_dp == 1:
        on_line(1, 0)
    from_peers(0, n_dp - 1)
    on_line(1, 1)
    from_sibling(0, 0, n_dp)
    x_out = pltpu.make_async_copy(xb, xo_ref, out_sem.at[0])
    x_out.start()
    weights[0].wait()
    weights[1].wait()
    steps = [(w, acc, k) for k in range(n_tensor) for w, acc in ((wg, gate), (wu, up))]
    done = 0
    for k in range(2, n_dp):
        upto = len(steps) * (k - 1) // (n_dp - 2)
        for w, acc, kk in steps[done:upto]:
            project(w, xb, acc, kk)
        done = upto
        on_line(1, k)
        from_peers(1, k - 2)
    for w, acc, kk in steps[done:]:
        project(w, xb, acc, kk)

    small = row_chunk(rows, 64)

    @pl.loop(0, rows // small)
    def _(i):
        r = pl.ds(pl.multiple_of(i * small, small), small)
        g, u = gate[r, :], up[r, :]
        sig = jax.nn.sigmoid(g)
        silu = g * sig
        hid_ref[r, :] = (silu * u).astype(jnp.bfloat16)
        gate[r, :] = u * sig * (1.0 + g * (1.0 - sig))
        up[r, :] = silu

    weights[2].wait()
    parts = 2 if n_dp % 2 == 0 and n_dp > 2 else 1
    size = n_dp // parts

    def backward(first):
        span = pl.ds(pl.multiple_of(first * unit, unit), size * unit)
        for i in range(rows // chunk):
            r = slice(i * chunk, (i + 1) * chunk)
            grad = lax.dot_general(
                wd[r, :depth], yb[0, span, :], NT, preferred_element_type=jnp.float32
            )
            for k in range(1, n_tensor):
                grad += lax.dot_general(
                    wd[r, k * depth:(k + 1) * depth], yb[k, span, :], NT,
                    preferred_element_type=jnp.float32,
                )
            gg_ref[r, span] = (grad * gate[r, span]).astype(jnp.bfloat16)
            gu_ref[r, span] = (grad * up[r, span]).astype(jnp.bfloat16)

    near = (z // size) * size
    if parts == 2:
        from_sibling(1, near, size)
        backward(near)
    from_peers(1, n_dp - 2)
    from_peers(1, n_dp - 1)
    far = size - near if parts == 2 else near
    from_sibling(1, far, size)
    y_out = pltpu.make_async_copy(yb, yo_ref, out_sem.at[1])
    y_out.start()
    backward(far)

    for wait in sent:
        wait()
    x_out.wait()
    y_out.wait()


def squares(count, seq, gg_ref, gu_ref, hid_ref, x_ref, y_ref, fg_ref, fu_ref, fd_ref):
    rows, columns = fg_ref.shape
    chunk = row_chunk(rows, 448)
    wide = 256 if columns % 256 == 0 else columns
    for act, grads, out in ((x_ref, gg_ref, fg_ref), (x_ref, gu_ref, fu_ref), (y_ref, hid_ref, fd_ref)):
        for q in range(columns // wide):
            for i in range(rows // chunk):
                r = slice(i * chunk, (i + 1) * chunk)
                total = None
                for e in range(count):
                    span = slice(e * seq, (e + 1) * seq)
                    g = jnp.dot(
                        grads[r, span], act[span, q * wide:(q + 1) * wide],
                        preferred_element_type=jnp.float32,
                    )
                    total = g * g if total is None else total + g * g
                out[r, q * wide:(q + 1) * wide] = total * (1.0 / count)


def local(n_dp, n_tensor, activations, out_grad, w_gate, w_up, w_down):
    per, seq, depth = activations.shape
    count = per * n_dp
    rows, features = w_gate.shape
    tokens = count * seq
    x = activations.reshape(per * seq, depth)
    y = out_grad.reshape(per * seq, depth)
    n_lines = n_tensor // 2
    blocks = jax.ShapeDtypeStruct((n_tensor, tokens, depth), jnp.bfloat16)
    grads = jax.ShapeDtypeStruct((rows, tokens), jnp.bfloat16)
    anywhere = pl.BlockSpec(memory_space=pl.ANY)
    in_vmem = pl.BlockSpec(memory_space=pltpu.VMEM)
    xb, yb, gg, gu, hid = pl.pallas_call(
        functools.partial(gather_forward, n_dp, n_tensor),
        out_shape=(blocks, blocks, grads, grads, grads),
        in_specs=[anywhere] * 5,
        out_specs=(anywhere, anywhere, in_vmem, in_vmem, in_vmem),
        scratch_shapes=[
            pltpu.VMEM(blocks.shape, jnp.bfloat16),
            pltpu.VMEM(blocks.shape, jnp.bfloat16),
            pltpu.VMEM((rows, features), jnp.bfloat16),
            pltpu.VMEM((rows, features), jnp.bfloat16),
            pltpu.VMEM((rows, features), jnp.bfloat16),
            pltpu.VMEM((rows, tokens), jnp.float32),
            pltpu.VMEM((rows, tokens), jnp.float32),
            pltpu.SemaphoreType.DMA((2,)),
            pltpu.SemaphoreType.DMA((3,)),
            pltpu.SemaphoreType.DMA((2, n_dp, n_tensor)),
            pltpu.SemaphoreType.DMA((2, n_dp, 1 + n_lines)),
            pltpu.SemaphoreType.DMA((2, n_dp, n_lines)),
            pltpu.SemaphoreType.DMA((n_lines,)),
            pltpu.SemaphoreType.DMA((2,)),
        ],
        compiler_params=pltpu.CompilerParams(
            collective_id=0, has_side_effects=True, vmem_limit_bytes=56 * 2**20
        ),
        name="gather_forward",
    )(x, y, w_gate, w_up, w_down)

    wide = min(depth, 512)
    per_block = depth // wide
    whole = pl.BlockSpec((rows, tokens), lambda i: (0, 0))
    act_spec = pl.BlockSpec((None, tokens, wide), lambda i: (i // per_block, 0, i % per_block))
    out_spec = pl.BlockSpec((rows, wide), lambda i: (0, i))
    fisher = jax.ShapeDtypeStruct((rows, features), jnp.float32)
    return pl.pallas_call(
        functools.partial(squares, count, seq),
        grid=(features // wide,),
        out_shape=(fisher, fisher, fisher),
        in_specs=[whole, whole, whole, act_spec, act_spec],
        out_specs=(out_spec, out_spec, out_spec),
        compiler_params=pltpu.CompilerParams(vmem_limit_bytes=56 * 2**20),
        name="squares",
    )(gg, gu, hid, xb, yb)


def solution(mesh):
    n_dp, n_tensor = mesh.shape["dp"], mesh.shape["tensor"]
    return jax.shard_map(
        functools.partial(local, n_dp, n_tensor),
        mesh=mesh,
        in_specs=(
            P(("parts", "dp"), None, "tensor"),
            P(("parts", "dp"), None, "tensor"),
            P(("parts", "dp", "tensor"), None),
            P(("parts", "dp", "tensor"), None),
            P(("parts", "dp", "tensor"), None),
        ),
        out_specs=(
            P(("parts", "dp", "tensor"), None),
            P(("parts", "dp", "tensor"), None),
            P(("parts", "dp", "tensor"), None),
        ),
        check_vma=False,
    )
```
